256 devices in a mesh: replica: 16 (over x_hi, z), fsdp: 16 (over y, x_lo, core).
Axes of the slice: x: 4 (x_hi: 2, x_lo: 2; x = x_hi * 2 + x_lo), y: 4, z: 8, core: 2. Of those that a mesh axis runs over, the one named last changes fastest.
Arguments:
- local_params: bfloat16 [16, 2048, 8192], P('replica', 'fsdp'), may hold values from -6 to 6
- global_params: bfloat16 [2048, 8192], P('fsdp'), may hold values from -6 to 6
- momentum: float32 [2048, 2048], P('fsdp'), may hold values from -4 to 4
- kept: int32 [32], replicated, may hold values from 0 to 31, as said below
Outputs:
- new_params: bfloat16 [2048, 8192], replicated
- new_momentum: float32 [2048, 2048], P('fsdp')
The draws below stay inside these ranges and needn't reach their ends.
Inputs may be any that keep to these rules, and one draw needn't show every extreme that they name: `kept`: a permutation of 0 to 31.
All inputs are finite; a program needn't handle non-finite values.
Results may differ from the reference program's by a relative error of at most 0.017.
Values may be sent and summed in bfloat16 or wider, within the bound.
A program may use at most 192 MiB of HBM per device.

```python
import jax
import jax.numpy as jnp
from jax import lax

D = 8192
BLOCK = 128
KEEP = 32
NB = 64
ROWS = 2048
REPLICAS = 16


def draw_kept(key, part):
    key = jax.random.fold_in(key, 1)
    return jax.random.permutation(key, KEEP).astype(jnp.int32)


def block_levels(rng, extent, shards, least, high):
    loudness = 1.0
    for position, shards_of in shards:
        heights = jax.random.uniform(jax.random.fold_in(jax.random.fold_in(rng, 6), position), (shards_of,), jnp.float32, least / len(shards), high / len(shards))
        loudness = loudness * jnp.repeat(jnp.exp(heights), extent[position] // shards_of).reshape((-1,) + (1,) * (len(extent) - 1 - position))
    return loudness


def centred(key, shape, spread, most, pieces=(), held_as=jnp.bfloat16):
    level = block_levels(key, shape, pieces, -0.22, 0.18) if pieces else 1.0
    array = jax.random.normal(key, shape, jnp.float32) * spread * level
    return jnp.minimum(jnp.maximum(array, -most), most).astype(held_as)


def setup_inputs(seed: int = 0) -> dict:
    key_list = jax.random.split(jax.random.key(seed), 5)
    local_params = centred(key_list[0], (REPLICAS, ROWS, D), 1.0, 6.0, ((0, 16), (1, 16)))
    global_params = centred(key_list[1], (ROWS, D), 1.0, 6.0, ((0, 16),))
    momentum = centred(key_list[2], (ROWS, NB * KEEP), 0.5, 4.0, ((0, 16),), jnp.float32)
    kept = draw_kept(jax.random.fold_in(key_list[4], 71), 0)
    return {"local_params": local_params, "global_params": global_params, "momentum": momentum, "kept": kept}


def make_basis(kept):
    freq = kept.astype(jnp.float32)[:, None]
    place = jnp.arange(BLOCK).astype(jnp.float32)[None, :]
    scale = jnp.where(kept[:, None] == 0, jnp.sqrt(1.0 / BLOCK), jnp.sqrt(2.0 / BLOCK)).astype(jnp.float32)
    return scale * jnp.cos(jnp.pi * (2.0 * place + 1.0) * freq / (2.0 * BLOCK))

def reference(local_params, global_params, momentum, kept):
    basis = make_basis(kept)
    glob = global_params.astype(jnp.float32)

    def one(total, local):
        delta = (glob - local.astype(jnp.float32)).reshape(ROWS, NB, BLOCK)
        coef = jnp.einsum('rbn,jn->rbj', delta, basis, precision=lax.Precision.HIGHEST)
        return (total + coef, None)
    total, _ = lax.scan(one, jnp.zeros((ROWS, NB, KEEP), jnp.float32), local_params)
    mean = total / REPLICAS
    new_mom = 0.9 * momentum.reshape(ROWS, NB, KEEP) + mean
    step = mean + 0.9 * new_mom
    update = jnp.einsum('rbj,jn->rbn', step, basis, precision=lax.Precision.HIGHEST).reshape(ROWS, D)
    new_params = (glob - 0.7 * update).astype(jnp.bfloat16)
    return (new_params, new_mom.reshape(ROWS, NB * KEEP))
```

```python
import jax
import jax.numpy as jnp
from jax import lax
from jax.experimental import pallas as pl
from jax.experimental.pallas import tpu as pltpu
from jax.sharding import PartitionSpec as P

D = 8192
BLOCK = 128
KEEP = 32
ROWS = 2048
SHARD = 128
NZ, NY, NX = 8, 4, 4
REPLICAS = 16
NQ = 4
RQ = SHARD // NQ
GROUPS = 16
GW = D // GROUPS
VMEM = 24 << 20
SPLIT = [(3584, 1536, 384)] * NQ


def here():
    r = lax.axis_index("replica")
    f = lax.axis_index("fsdp")
    x = (r // NZ) * 2 + lax.rem(f // 2, 2)
    return x, f // 4, lax.rem(r, NZ), lax.rem(f, 2)


def device(x, y, z, c):
    x = lax.rem(x + NX, NX)
    y = lax.rem(y + NY, NY)
    z = lax.rem(z + NZ, NZ)
    return ((x // 2) * NZ + z, y * 4 + lax.rem(x, 2) * 2 + c)


def block_mask(shape, row_width, column_width):
    rows = lax.broadcasted_iota(jnp.int32, shape, 0) // row_width
    columns = lax.broadcasted_iota(jnp.int32, shape, 1) // column_width
    return rows == columns


def make_bases(kept_ref, forward, inverse):
    freq = jnp.broadcast_to(kept_ref[...], (BLOCK, 4 * KEEP))
    place = lax.broadcasted_iota(jnp.int32, (BLOCK, 4 * KEEP), 0)
    turn = ((2 * place + 1) * freq) & (4 * BLOCK - 1)
    angle = turn.astype(jnp.float32) * (jnp.pi / (2 * BLOCK))
    scale = jnp.where(freq == 0, (1.0 / BLOCK) ** 0.5, (2.0 / BLOCK) ** 0.5).astype(jnp.float32)
    basis = scale * jnp.cos(angle)
    wide = jnp.concatenate([basis] * 4, axis=0)
    wide = jnp.where(block_mask(wide.shape, BLOCK, KEEP), wide, 0.0)
    high = wide.astype(jnp.bfloat16)
    forward[:, : 4 * KEEP] = high
    forward[:, 4 * KEEP :] = (wide - high.astype(jnp.float32)).astype(jnp.bfloat16)
    back = jnp.concatenate([basis.T * 0.7] * 4, axis=1)
    back = jnp.where(block_mask(back.shape, KEEP, BLOCK), back, 0.0)
    high = back.astype(jnp.bfloat16)
    inverse[: 4 * KEEP, :] = high
    inverse[4 * KEEP :, :] = (back - high.astype(jnp.float32)).astype(jnp.bfloat16)


def outer_kernel(local_ref, glob_ref, mom_in, kept_ref, T, new_mom,
                 lbuf, gbuf, mom, forward, inverse, lhs, coefs, parts, swap_out, swap_in, means,
                 load_sem, send_sem, recv_sem):
    x, y, z, c = here()
    count = [0]
    all_copies = []

    def remote(src, dst, to, landing=None):
        i = count[0]
        count[0] += 1
        copy = pltpu.make_async_remote_copy(
            src, dst, send_sem.at[i], recv_sem.at[i], device_id=to
        )
        copy.start()
        all_copies.append(copy)
        if landing is None:
            return copy
        return pltpu.make_async_remote_copy(
            src, landing, send_sem.at[i], recv_sem.at[i], device_id=to
        )

    def arrive(copies):
        for copy in copies:
            copy.wait_recv()

    sibling = device(x, y, z, 1 - c)
    up, down = device(x, y + 1, z, c), device(x, y - 1, z, c)
    right, left = device(x + 1, y, z, c), device(x - 1, y, z, c)
    far = device(x + 2, y, z, c)
    along = [device(x, y, z + d, c) for d in range(NZ)]
    ahead, behind = along[1], along[NZ - 1]
    barrier = pltpu.get_barrier_semaphore()
    peers = along[1:] + [far, up, down, right, left, sibling]
    for peer in peers:
        pl.semaphore_signal(barrier, inc=1, device_id=peer)

    loads = []
    for q in range(NQ):
        rows = pl.ds(q * RQ, RQ)
        pair = [
            pltpu.make_async_copy(local_ref.at[0, rows], lbuf.at[rows], load_sem.at[2 * q]),
            pltpu.make_async_copy(glob_ref.at[rows], gbuf.at[rows], load_sem.at[2 * q + 1]),
        ]
        for copy in pair:
            copy.start()
        loads.append(pair)
    mom_load = pltpu.make_async_copy(mom_in, mom, load_sem.at[2 * NQ])
    mom_load.start()
    make_bases(kept_ref, forward, inverse)

    st = [dict() for _ in range(NQ)]

    def zi(k):
        return lax.rem(z + k + 2 * NZ, NZ)

    def coefficients(q):
        for copy in loads[q]:
            copy.wait()
        rows = pl.ds(q * RQ, RQ)
        for i in range(GROUPS):
            g = (i % 2) * NZ + i // 2
            cols = pl.ds(g * GW, GW)
            delta = gbuf[rows, cols].astype(jnp.float32) - lbuf[rows, cols].astype(jnp.float32)
            lhs[pl.ds(i * RQ, RQ), :] = delta.astype(jnp.bfloat16)
        both = jnp.dot(lhs[...], forward[...], preferred_element_type=jnp.float32)
        coef = both[:, : 4 * KEEP] + both[:, 4 * KEEP :]
        coefs[q] = coef.astype(jnp.bfloat16).reshape(NZ, 2, RQ, 4 * KEEP)
        if q == 0:
            pl.semaphore_wait(barrier, len(peers))
        st[q]["rs"] = [
            remote(coefs.at[q, zi(d)], parts.at[q, d], along[d]) for d in range(1, NZ)
        ]

    def partial_sum(q):
        arrive(st[q]["rs"])
        total = coefs[q, z].astype(jnp.float32)
        for d in range(1, NZ):
            total = total + parts[q, d].astype(jnp.float32)
        swap_out[q] = total.astype(jnp.bfloat16)
        st[q]["swap"] = [remote(swap_out.at[q], swap_in.at[q], far)]

    def mean(q):
        arrive(st[q]["swap"])
        total = swap_out[q].astype(jnp.float32) + swap_in[q].astype(jnp.float32)
        means[q, z] = (total * (1.0 / REPLICAS)).astype(jnp.bfloat16)
        st[q]["mean"] = [
            remote(means.at[q, z], means.at[q, z], along[d], means.at[q, zi(-d)])
            for d in range(1, NZ)
        ]

    def new_rows(q):
        arrive(st[q]["mean"])
        if q == 0:
            mom_load.wait()
        rows = pl.ds(q * RQ, RQ)
        steps = []
        for i in range(GROUPS):
            g = (i % 2) * NZ + i // 2
            cols = pl.ds(g * 4 * KEEP, 4 * KEEP)
            avg = means[q, i // 2, i % 2].astype(jnp.float32)
            fresh = 0.9 * mom[rows, cols] + avg
            new_mom[rows, cols] = fresh
            step = (avg + 0.9 * fresh).astype(jnp.bfloat16)
            lhs[pl.ds(i * RQ, RQ), : 4 * KEEP] = step
            lhs[pl.ds(i * RQ, RQ), 4 * KEEP : 8 * KEEP] = step
        update = jnp.dot(lhs[:, : 8 * KEEP], inverse[...], preferred_element_type=jnp.float32)
        for i in range(GROUPS):
            g = (i % 2) * NZ + i // 2
            cols = pl.ds(g * GW, GW)
            mine = gbuf[rows, cols].astype(jnp.float32) - update[i * RQ : (i + 1) * RQ]
            T[0, 0, 0, rows, cols] = mine.astype(jnp.bfloat16)

    def geometry(q):
        a1, a2, b = SPLIT[q]
        a = a1 + a2
        rows = pl.ds(q * RQ, RQ)
        first, second = pl.ds(q * RQ, RQ // 2), pl.ds(q * RQ + RQ // 2, RQ // 2)
        def strip(k):
            return pl.ds(pl.multiple_of(a + zi(k) * b, 128), b)
        return a1, a2, a, b, rows, first, second, strip

    def g0(q):
        a1, a2, a, b, rows, first, second, strip = geometry(q)
        every, h0, h1, s = pl.ds(0, a), pl.ds(0, a // 2), pl.ds(a // 2, a // 2), strip(0)
        s_ = st[q]
        s_["y1"] = [
            remote(T.at[0, 0, 0, rows, every], T.at[0, 3, 0, rows, every], up),
            remote(T.at[0, 0, 0, rows, every], T.at[0, 1, 0, rows, every], down),
        ]
        s_["x1"] = [
            remote(T.at[0, 0, 0, rows, h0], T.at[0, 0, 1, rows, h0], right),
            remote(T.at[0, 0, 0, rows, h1], T.at[0, 0, 1, rows, h1], left),
        ]
        if b:
            s_["y1"] += [
                remote(T.at[0, 0, 0, rows, s], T.at[0, 3, 0, rows, s], up),
                remote(T.at[0, 0, 0, rows, s], T.at[0, 1, 0, rows, s], down),
            ]
            s_["bx1"] = [
                remote(T.at[0, 0, 0, first, s], T.at[0, 0, 1, first, s], right),
                remote(T.at[0, 0, 0, second, s], T.at[0, 0, 1, second, s], left),
            ]
        s_["d2d"] = [remote(T.at[0, 0, 0, rows], T.at[1, 0, 0, rows], sibling)]

    def g1(q):
        a1, a2, a, b, rows, first, second, strip = geometry(q)
        h0, h1, s = pl.ds(0, a // 2), pl.ds(a // 2, a // 2), strip(0)
        mid = pl.ds(a1 // 2, a2)
        s_ = st[q]
        arrive(s_["y1"])
        s_["y2"] = [
            remote(T.at[0, 3, 0, rows, h0], T.at[0, 2, 0, rows, h0], up),
            remote(T.at[0, 1, 0, rows, h1], T.at[0, 2, 0, rows, h1], down),
        ]
        if b:
            s_["y2"] += [
                remote(T.at[0, 3, 0, first, s], T.at[0, 2, 0, first, s], up),
                remote(T.at[0, 1, 0, second, s], T.at[0, 2, 0, second, s], down),
            ]
        arrive(s_["x1"])
        s_["xy1"] = []
        if a2:
            s_["xy1"] = [
                remote(T.at[0, 0, 1, rows, mid], T.at[0, 3, 1, rows, mid], up),
                remote(T.at[0, 0, 1, rows, mid], T.at[0, 1, 1, rows, mid], down),
            ]

    def g2(q):
        a1, a2, a, b, rows, first, second, strip = geometry(q)
        s = strip(0)
        o0, o1 = pl.ds(0, a1 // 2), pl.ds(a1 // 2 + a2, a1 // 2)
        m0, m1 = pl.ds(a1 // 2, a2 // 2), pl.ds(a1 // 2 + a2 // 2, a2 // 2)
        three = pl.ds(1, 3)
        s_ = st[q]
        arrive(s_["y2"])
        s_["x2"] = [
            remote(T.at[0, three, 0, rows, o0], T.at[0, three, 1, rows, o0], right),
            remote(T.at[0, three, 0, rows, o1], T.at[0, three, 1, rows, o1], left),
        ]
        if b:
            s_["bx2"] = [
                remote(T.at[0, three, 0, first, s], T.at[0, three, 1, first, s], right),
                remote(T.at[0, three, 0, second, s], T.at[0, three, 1, second, s], left),
            ]
        arrive(s_["xy1"])
        s_["xy2"] = []
        if a2:
            s_["xy2"] = [
                remote(T.at[0, 3, 1, rows, m0], T.at[0, 2, 1, rows, m0], up),
                remote(T.at[0, 1, 1, rows, m1], T.at[0, 2, 1, rows, m1], down),
            ]
        every = pl.ds(0, a)
        s_["d2d"] += [
            remote(T.at[0, three, 0, rows, every], T.at[1, three, 0, rows, every], sibling)
        ]

    pieces = [(0, 1), (pl.ds(1, 3), slice(None))]

    def z_hop(q, hop):
        a1, a2, a, b, rows, first, second, strip = geometry(q)
        out = []
        for dy, dx in pieces:
            for to, sign in ((ahead, -1), (behind, 1)):
                r = rows if hop < 3 else (first if sign < 0 else second)
                s = strip(sign * hop)
                land = strip(sign * (hop + 1))
                out.append(remote(T.at[0, dy, dx, r, s], T.at[0, dy, dx, r, s], to,
                                  T.at[0, dy, dx, r, land]))
        st[q]["z%d" % hop] = out

    def g3(q):
        a1, a2, a, b, rows, first, second, strip = geometry(q)
        s_ = st[q]
        if b:
            arrive(s_["bx1"] + s_["bx2"])
            z_hop(q, 0)
        arrive(s_["x2"] + s_["xy2"])
        every = pl.ds(0, a)
        s_["d2d"] += [remote(T.at[0, :, 1, rows, every], T.at[1, :, 1, rows, every], sibling)]

    def later_hop(hop):
        def go(q):
            if SPLIT[q][2]:
                arrive(st[q]["z%d" % (hop - 1)])
                z_hop(q, hop)
        return go

    def g7(q):
        a1, a2, a, b, rows, first, second, strip = geometry(q)
        if b:
            arrive(st[q]["z3"])
            rest = pl.ds(a, D - a)
            st[q]["d2d"] += [
                remote(T.at[0, dy, dx, rows, rest], T.at[1, dy, dx, rows, rest], sibling)
                for dy, dx in pieces
            ]

    def finish(q):
        arrive(st[q]["d2d"])

    first_part = [coefficients, partial_sum, mean]
    second_part = [lambda q: (new_rows(q), g0(q)), g1, g2, g3] + [later_hop(h) for h in (1, 2, 3)] + [g7]
    stages = first_part + second_part
    for wave in range(len(stages) + NQ - 1):
        for q in reversed(range(NQ)):
            k = wave - q
            if 0 <= k < len(stages):
                stages[k](q)
    for q in range(NQ):
        finish(q)
    for copy in all_copies:
        copy.wait_send()


NSEM = 64 * NQ


def place_kernel(T, mom, params, new_mom, sem):
    x, y, z, c = here()
    copies = [pltpu.make_async_copy(mom, new_mom, sem.at[16])]
    for p in range(2):
        for dy in range(4):
            for dx in range(2):
                shard = (
                    lax.rem(y + dy, NY) * 4 + lax.rem(x + dx, 2) * 2 + lax.rem(c + p, 2)
                )
                rows = pl.ds(pl.multiple_of(shard * SHARD, SHARD), SHARD)
                copies.append(
                    pltpu.make_async_copy(
                        T.at[p, dy, dx], params.at[rows], sem.at[(p * 4 + dy) * 2 + dx]
                    )
                )
    for copy in copies:
        copy.start()
    for copy in copies:
        copy.wait()


def on_device(local_params, global_params, momentum, kept):
    lanes = jnp.tile(kept, 4)[None, :]
    bf16, f32 = jnp.bfloat16, jnp.float32
    anywhere = pl.BlockSpec(memory_space=pl.ANY)
    in_vmem = pl.BlockSpec(memory_space=pltpu.VMEM)
    T, mom = pl.pallas_call(
        outer_kernel,
        out_shape=(pltpu.VMEM((2, 4, 2, SHARD, D), bf16), pltpu.VMEM((SHARD, D // 4), f32)),
        in_specs=[anywhere, anywhere, anywhere, in_vmem],
        out_specs=(in_vmem, in_vmem),
        scratch_shapes=[
            pltpu.VMEM((SHARD, D), bf16),
            pltpu.VMEM((SHARD, D), bf16),
            pltpu.VMEM((SHARD, D // 4), f32),
            pltpu.VMEM((GW, 8 * KEEP), bf16),
            pltpu.VMEM((8 * KEEP, GW), bf16),
            pltpu.VMEM((GROUPS * RQ, GW), bf16),
            pltpu.VMEM((NQ, NZ, 2, RQ, 4 * KEEP), bf16),
            pltpu.VMEM((NQ, NZ, 2, RQ, 4 * KEEP), bf16),
            pltpu.VMEM((NQ, 2, RQ, 4 * KEEP), bf16),
            pltpu.VMEM((NQ, 2, RQ, 4 * KEEP), bf16),
            pltpu.VMEM((NQ, NZ, 2, RQ, 4 * KEEP), bf16),
            pltpu.SemaphoreType.DMA((2 * NQ + 1,)),
            pltpu.SemaphoreType.DMA((NSEM,)),
            pltpu.SemaphoreType.DMA((NSEM,)),
        ],
        compiler_params=pltpu.CompilerParams(
            collective_id=0, has_side_effects=True, vmem_limit_bytes=VMEM
        ),
    )(local_params, global_params, momentum, lanes)
    return pl.pallas_call(
        place_kernel,
        out_shape=(
            jax.ShapeDtypeStruct((ROWS, D), bf16),
            jax.ShapeDtypeStruct((SHARD, D // 4), f32),
        ),
        in_specs=[in_vmem, in_vmem],
        out_specs=(anywhere, anywhere),
        scratch_shapes=[pltpu.SemaphoreType.DMA((17,))],
        compiler_params=pltpu.CompilerParams(vmem_limit_bytes=VMEM),
    )(
        pltpu.with_memory_space_constraint(T, pltpu.VMEM),
        pltpu.with_memory_space_constraint(mom, pltpu.VMEM),
    )


def solution(mesh):
    in_specs = (P("replica", "fsdp", None), P("fsdp", None), P("fsdp", None), P())
    out_specs = (P(), P("fsdp", None))
    return jax.shard_map(
        on_device, mesh=mesh, in_specs=in_specs, out_specs=out_specs, check_vma=False
    )
```

```python
import jax
import jax.numpy as jnp
from jax import lax
from jax.experimental import pallas as pl
from jax.experimental.pallas import tpu as pltpu
from jax.sharding import PartitionSpec as P

D = 8192
BLOCK = 128
KEEP = 32
ROWS = 2048
SHARD = 128
NZ, NY, NX = 8, 4, 4
REPLICAS = 16
GROUPS = 16
GW = D // GROUPS
VMEM = 24 << 20
CHUNKS = [(0, 32), (32, 32), (64, 32), (96, 32)]
NQ = len(CHUNKS)
SPLIT = [(3072, 0, 640), (5120, 0, 384), (4608, 2560, 128), (4864, 2304, 128)]
SEMAPHORES = 190
ORDER = [
    ("coef", 0), ("coef", 1), ("coef", 2), ("sum", 0), ("coef", 3), ("sum", 1), ("mean", 0), ("sum", 2),
    ("mean", 1), ("sum", 3), ("mean", 2), ("rows", 0), ("oyB", 0), ("ox1", 0), ("oxB", 0), ("oy", 0), ("od", 0),
    ("rows", 1), ("yB2", 0), ("oyB", 1), ("ox1", 1), ("oxB", 1), ("oy", 1), ("od", 1), ("mean", 3), ("rows", 2),
    ("xB2", 0), ("x2a", 0), ("yB2", 1), ("oxB", 2), ("oy", 2), ("od", 2), ("rows", 3), ("z0", 0), ("oxB", 3),
    ("oy", 3), ("od", 3), ("ox2", 2), ("xB2", 1), ("x2a", 1), ("ay1", 2), ("z0", 1), ("z1", 0), ("x2a", 2),
    ("z1", 1), ("oyB", 2), ("oyB", 3), ("x2a", 3), ("y2", 0), ("z2", 0), ("y2", 1), ("yB2", 2), ("yB2", 3),
    ("x2b", 0), ("d1", 0), ("z2", 1), ("ay0", 2), ("xB2", 3), ("x2b", 1), ("d1", 1), ("xB2", 2), ("y2", 2),
    ("z3", 0), ("d2", 0), ("ay2", 2), ("ox1", 2), ("z3", 1), ("x2b", 2), ("d1", 2), ("ay0", 3), ("d2", 1),
    ("z0", 2), ("z0", 3), ("d3", 2), ("y2", 3), ("ox2", 3), ("d4", 1), ("ox1", 3), ("d4", 0), ("d2", 2),
    ("z1", 2), ("z1", 3), ("ay1", 3), ("x2b", 3), ("d1", 3), ("z2", 2), ("z2", 3), ("z3", 2), ("ay2", 3),
    ("z3", 3), ("d2", 3), ("d4", 2), ("d4", 3), ("d3", 3),
]


def here():
    r = lax.axis_index("replica")
    f = lax.axis_index("fsdp")
    x = (r // NZ) * 2 + lax.rem(f // 2, 2)
    return x, f // 4, lax.rem(r, NZ), lax.rem(f, 2)


def device(x, y, z, c):
    x = lax.rem(x + NX, NX)
    y = lax.rem(y + NY, NY)
    z = lax.rem(z + NZ, NZ)
    return ((x // 2) * NZ + z, y * 4 + lax.rem(x, 2) * 2 + c)


def block_mask(shape, row_width, column_width):
    rows = lax.broadcasted_iota(jnp.int32, shape, 0) // row_width
    columns = lax.broadcasted_iota(jnp.int32, shape, 1) // column_width
    return rows == columns


def make_bases(kept_ref, forward, inverse):
    lanes = jnp.concatenate([kept_ref[...]] * 4, axis=1)
    freq = jnp.broadcast_to(lanes, (BLOCK, 4 * KEEP))
    place = lax.broadcasted_iota(jnp.int32, (BLOCK, 4 * KEEP), 0)
    turn = ((2 * place + 1) * freq) & (4 * BLOCK - 1)
    angle = turn.astype(jnp.float32) * (jnp.pi / (2 * BLOCK))
    scale = jnp.where(freq == 0, (1.0 / BLOCK) ** 0.5, (2.0 / BLOCK) ** 0.5).astype(jnp.float32)
    basis = scale * jnp.cos(angle)
    wide = jnp.concatenate([basis] * 4, axis=0)
    wide = jnp.where(block_mask(wide.shape, BLOCK, KEEP), wide, 0.0)
    high = wide.astype(jnp.bfloat16)
    forward[:, : 4 * KEEP] = high
    forward[:, 4 * KEEP :] = (wide - high.astype(jnp.float32)).astype(jnp.bfloat16)
    back = jnp.concatenate([basis.T * 0.7] * 4, axis=1)
    back = jnp.where(block_mask(back.shape, KEEP, BLOCK), back, 0.0)
    high = back.astype(jnp.bfloat16)
    inverse[: 4 * KEEP, :] = high
    inverse[4 * KEEP :, :] = (back - high.astype(jnp.float32)).astype(jnp.bfloat16)


def outer_kernel(local_ref, glob_ref, mom_in, kept_ref, T, new_mom,
                 lbuf, gbuf, mom, forward, inverse, lhs, coefs, parts, swap_out, swap_in, means,
                 load_sem, send_sem, recv_sem):
    x, y, z, c = here()
    all_copies = []

    def remote(src, dst, to, landing=None):
        i = len(all_copies)
        copy = pltpu.make_async_remote_copy(
            src, dst, send_sem.at[i], recv_sem.at[i], device_id=to
        )
        copy.start()
        all_copies.append(copy)
        if landing is None:
            return copy
        return pltpu.make_async_remote_copy(
            src, landing, send_sem.at[i], recv_sem.at[i], device_id=to
        )

    flying = {}

    def arrive(*names):
        for name in names:
            for copy in flying.pop(name, []):
                copy.wait_recv()

    sibling = device(x, y, z, 1 - c)
    up, down = device(x, y + 1, z, c), device(x, y - 1, z, c)
    right, left = device(x + 1, y, z, c), device(x - 1, y, z, c)
    far = device(x + 2, y, z, c)
    along = [device(x, y, z + d, c) for d in range(NZ)]
    ahead, behind = along[1], along[NZ - 1]
    barrier = pltpu.get_barrier_semaphore()
    peers = along[1:] + [far, up, down, right, left, sibling]
    for peer in peers:
        pl.semaphore_signal(barrier, inc=1, device_id=peer)

    loads = []
    for q, (start, size) in enumerate(CHUNKS):
        rows = pl.ds(start, size)
        pair = [
            pltpu.make_async_copy(local_ref.at[0, rows], lbuf.at[rows], load_sem.at[2 * q]),
            pltpu.make_async_copy(glob_ref.at[rows], gbuf.at[rows], load_sem.at[2 * q + 1]),
        ]
        for copy in pair:
            copy.start()
        loads.append(pair)
    mom_load = pltpu.make_async_copy(mom_in, mom, load_sem.at[2 * NQ])
    mom_load.start()
    make_bases(kept_ref, forward, inverse)

    def zi(k):
        return lax.rem(z + k + 2 * NZ, NZ)

    def column_group(i):
        return (i % 2) * NZ + i // 2

    def coef(q):
        for copy in loads[q]:
            copy.wait()
        start, size = CHUNKS[q]
        rows = pl.ds(start, size)
        for i in range(GROUPS):
            cols = pl.ds(column_group(i) * GW, GW)
            delta = gbuf[rows, cols].astype(jnp.float32) - lbuf[rows, cols].astype(jnp.float32)
            lhs[pl.ds(i * size, size), :] = delta.astype(jnp.bfloat16)
        both = jnp.dot(
            lhs[: GROUPS * size], forward[...], preferred_element_type=jnp.float32
        )
        out = both[:, : 4 * KEEP] + both[:, 4 * KEEP :]
        coefs[:, :, rows] = out.astype(jnp.bfloat16).reshape(NZ, 2, size, 4 * KEEP)
        if q == 0:
            pl.semaphore_wait(barrier, len(peers))
        return [
            remote(coefs.at[zi(d), :, rows], parts.at[d, :, rows], along[d])
            for d in range(1, NZ)
        ]

    def partial_sum(q):
        arrive(("coef", q))
        rows = pl.ds(*CHUNKS[q])
        total = coefs[z, :, rows].astype(jnp.float32)
        for d in range(1, NZ):
            total = total + parts[d, :, rows].astype(jnp.float32)
        swap_out[:, rows] = total.astype(jnp.bfloat16)
        return [remote(swap_out.at[:, rows], swap_in.at[:, rows], far)]

    def mean(q):
        arrive(("sum", q))
        rows = pl.ds(*CHUNKS[q])
        total = swap_out[:, rows].astype(jnp.float32) + swap_in[:, rows].astype(jnp.float32)
        means[z, :, rows] = (total * (1.0 / REPLICAS)).astype(jnp.bfloat16)
        return [
            remote(means.at[z, :, rows], means.at[z, :, rows], along[d],
                   means.at[zi(-d), :, rows])
            for d in range(1, NZ)
        ]

    def new_rows(q):
        arrive(("mean", q))
        if q == 0:
            mom_load.wait()
        start, size = CHUNKS[q]
        rows = pl.ds(start, size)
        for i in range(GROUPS):
            cols = pl.ds(column_group(i) * 4 * KEEP, 4 * KEEP)
            avg = means[i // 2, i % 2, rows].astype(jnp.float32)
            fresh = 0.9 * mom[rows, cols] + avg
            new_mom[rows, cols] = fresh
            step = (avg + 0.9 * fresh).astype(jnp.bfloat16)
            lhs[pl.ds(i * size, size), : 4 * KEEP] = step
            lhs[pl.ds(i * size, size), 4 * KEEP : 8 * KEEP] = step
        update = jnp.dot(
            lhs[: GROUPS * size, : 8 * KEEP], inverse[...], preferred_element_type=jnp.float32
        )
        for i in range(GROUPS):
            cols = pl.ds(column_group(i) * GW, GW)
            mine = gbuf[rows, cols].astype(jnp.float32) - update[i * size : (i + 1) * size]
            T[0, 0, rows, cols] = mine.astype(jnp.bfloat16)
        return []

    def pass_on(q, name):
        a1, a2, b = SPLIT[q]
        a = a1 + a2
        rows = pl.ds(*CHUNKS[q])
        odd = q % 2
        p, p0, p1 = pl.ds(0, a1), pl.ds(0, a1 // 2), pl.ds(a1 // 2, a1 // 2)
        s, s0, s1 = pl.ds(a1, a2), pl.ds(a1, a2 // 2), pl.ds(a1 + a2 // 2, a2 // 2)

        def strip(k):
            return pl.ds(pl.multiple_of(a + zi(k) * b, 128), b)

        def send(slot, to_slot, cols, to, landing=None):
            return remote(
                T.at[0, slot, rows, cols], T.at[0, to_slot, rows, cols], to,
                None if landing is None else T.at[0, to_slot, rows, landing],
            )

        def share(slot, cols):
            return [remote(T.at[0, slot, rows, cols], T.at[1, slot, rows, cols], sibling)]

        near, away = pl.ds(1, 3), pl.ds(5, 3)
        others = pl.ds(1, 7)
        if name == "ox1":
            return [send(0, 4, p0, right), send(0, 4, p1, left)]
        if name == "oy":
            return [send(0, 3, p, up), send(0, 1, p, down)]
        if name == "od":
            return share(0, pl.ds(0, D))
        if name == "y2":
            arrive(("oy", q))
            return [send(3, 2, p0, up), send(1, 2, p1, down)]
        if name == "x2a":
            arrive(("oy", q))
            return [send(i, i + 4, h, to) for i in (1, 3) for h, to in ((p0, right), (p1, left))]
        if name == "x2b":
            arrive(("y2", q))
            return [send(2, 6, p0, right), send(2, 6, p1, left)]
        if name == "d1":
            arrive(("oy", q), ("y2", q))
            return share(near, p)
        if name == "d2":
            arrive(("ox1", q), ("x2a", q), ("x2b", q))
            return share(pl.ds(4, 4), p)
        if name == "ox2":
            return [send(0, 4, s0, right), send(0, 4, s1, left)]
        if name == "ay0":
            return [send(0, 3, s, up), send(0, 1, s, down)]
        if name == "ay1":
            arrive(("ox2", q))
            return [send(4, 7, s, up), send(4, 5, s, down)]
        if name == "ay2":
            arrive(("ay0", q), ("ay1", q))
            return [send(3, 2, s, up), send(5, 6, s, down)]
        if name == "d3":
            arrive(("ay2", q))
            return share(others, s)
        mine = strip(0)
        if name == "oyB":
            return [send(0, 3, mine, up), send(0, 1, mine, down)]
        if name == "oxB":
            return [send(0, 4, mine, right if odd else left)]
        if name == "yB2":
            arrive(("oyB", q))
            return [send(1, 2, mine, down) if odd else send(3, 2, mine, up)]
        if name == "xB2":
            arrive(("yB2", q))
            return [send(near, away, mine, left if odd else right)]
        if name == "d4":
            arrive(("z3", q))
            return share(others, pl.ds(a, D - a))
        hop = int(name[1])
        arrive(*((("xB2", q), ("oxB", q)) if hop == 0 else (("z%d" % (hop - 1), q),)))
        onward = [
            (strip(-hop), ahead, strip(-hop - 1)),
            (strip(hop), behind, strip(hop + 1)),
        ]
        if hop == 3:
            onward = onward[odd : odd + 1]
        return [send(others, others, cols, to, landing) for cols, to, landing in onward]

    compute = {"coef": coef, "sum": partial_sum, "mean": mean, "rows": new_rows}
    for name, q in ORDER:
        if name in compute:
            flying[name, q] = compute[name](q)
        else:
            flying[name, q] = pass_on(q, name)
    arrive(*list(flying))
    for copy in all_copies:
        copy.wait_send()


def place_kernel(T, mom, params, new_mom, sem):
    x, y, z, c = here()
    copies = [pltpu.make_async_copy(mom, new_mom, sem.at[16])]
    for p in range(2):
        for dy in range(4):
            for dx in range(2):
                slot = dx * 4 + dy
                shard = (
                    lax.rem(y + dy, NY) * 4 + lax.rem(x + dx, 2) * 2 + lax.rem(c + p, 2)
                )
                rows = pl.ds(pl.multiple_of(shard * SHARD, SHARD), SHARD)
                copies.append(
                    pltpu.make_async_copy(
                        T.at[p, slot], params.at[rows], sem.at[p * 8 + slot]
                    )
                )
    for copy in copies:
        copy.start()
    for copy in copies:
        copy.wait()


def on_device(local_params, global_params, momentum, kept):
    lanes = kept[None, :]
    bf16, f32 = jnp.bfloat16, jnp.float32
    anywhere = pl.BlockSpec(memory_space=pl.ANY)
    in_vmem = pl.BlockSpec(memory_space=pltpu.VMEM)
    T, mom = pl.pallas_call(
        outer_kernel,
        out_shape=(pltpu.VMEM((2, 8, SHARD, D), bf16), pltpu.VMEM((SHARD, D // 4), f32)),
        in_specs=[anywhere, anywhere, anywhere, in_vmem],
        out_specs=(in_vmem, in_vmem),
        scratch_shapes=[
            pltpu.VMEM((SHARD, D), bf16),
            pltpu.VMEM((SHARD, D), bf16),
            pltpu.VMEM((SHARD, D // 4), f32),
            pltpu.VMEM((GW, 8 * KEEP), bf16),
            pltpu.VMEM((8 * KEEP, GW), bf16),
            pltpu.VMEM((GROUPS * max(size for _, size in CHUNKS), GW), bf16),
            pltpu.VMEM((NZ, 2, SHARD, 4 * KEEP), bf16),
            pltpu.VMEM((NZ, 2, SHARD, 4 * KEEP), bf16),
            pltpu.VMEM((2, SHARD, 4 * KEEP), bf16),
            pltpu.VMEM((2, SHARD, 4 * KEEP), bf16),
            pltpu.VMEM((NZ, 2, SHARD, 4 * KEEP), bf16),
            pltpu.SemaphoreType.DMA((2 * NQ + 1,)),
            pltpu.SemaphoreType.DMA((SEMAPHORES,)),
            pltpu.SemaphoreType.DMA((SEMAPHORES,)),
        ],
        compiler_params=pltpu.CompilerParams(
            collective_id=0, has_side_effects=True, vmem_limit_bytes=VMEM
        ),
    )(local_params, global_params, momentum, lanes)
    return pl.pallas_call(
        place_kernel,
        out_shape=(
            jax.ShapeDtypeStruct((ROWS, D), bf16),
            jax.ShapeDtypeStruct((SHARD, D // 4), f32),
        ),
        in_specs=[in_vmem, in_vmem],
        out_specs=(anywhere, anywhere),
        scratch_shapes=[pltpu.SemaphoreType.DMA((17,))],
        compiler_params=pltpu.CompilerParams(vmem_limit_bytes=VMEM),
    )(
        pltpu.with_memory_space_constraint(T, pltpu.VMEM),
        pltpu.with_memory_space_constraint(mom, pltpu.VMEM),
    )


def solution(mesh):
    in_specs = (P("replica", "fsdp", None), P("fsdp", None), P("fsdp", None), P())
    out_specs = (P(), P("fsdp", None))
    return jax.shard_map(
        on_device, mesh=mesh, in_specs=in_specs, out_specs=out_specs, check_vma=False
    )
```

```python
import jax
import jax.numpy as jnp
from jax import lax
from jax.experimental import pallas as pl
from jax.experimental.pallas import tpu as pltpu
from jax.sharding import PartitionSpec as P

D = 8192
BLOCK = 128
KEEP = 32
ROWS = 2048
SHARD = 128
NZ, NY, NX = 8, 4, 4
REPLICAS = 16
GROUPS = 16
GW = D // GROUPS
VMEM = 24 << 20
CHUNKS = [(0, 48), (48, 16), (64, 32), (96, 32)]
NQ = len(CHUNKS)
SPLIT = {0: (2048, 0, 0), 1: (5120, 0, 384), 2: (4608, 1536, 256), 3: (3840, 1280, 384), 'raw': (2560, 3584, 256)}
SHARES = ("od", "d1", "d2", "d3", "d4")
SEMAPHORES = 214
ORDER = [
    ("load", "raw"), ("ox1", "raw"), ("oyB", "raw"), ("od", "raw"), ("oxB", "raw"), ("ay0", "raw"),
    ("ox2", "raw"), ("coef", 3), ("coef", 2), ("yB2", "raw"), ("coef", 1), ("coef", 0), ("oy", "raw"),
    ("sum", 3), ("xB2", "raw"), ("sum", 2), ("ay1", "raw"), ("sum", 1), ("mean", 3), ("z0", "raw"),
    ("x2a", "raw"), ("mean", 2), ("sum", 0), ("mean", 1), ("y2", "raw"), ("rows", 3), ("ox1", 3), ("oyB", 3),
    ("od", 3), ("oxB", 3), ("ox2", 3), ("ay0", 3), ("oy", 3), ("z1", "raw"), ("d1", "raw"), ("x2b", "raw"),
    ("mean", 0), ("yB2", 3), ("rows", 2), ("ox1", 2), ("oyB", 2), ("od", 2), ("oxB", 2), ("ox2", 2),
    ("rows", 1), ("oyB", 1), ("od", 1), ("oxB", 1), ("oy", 2), ("z2", "raw"), ("d2", "raw"), ("ox1", 1),
    ("xB2", 3), ("yB2", 2), ("yB2", 1), ("x2a", 3), ("oy", 1), ("rows", 0), ("od", 0), ("z0", 3), ("z3", "raw"),
    ("oy", 0), ("xB2", 1), ("xB2", 2), ("ox1", 0), ("x2a", 2), ("z0", 2), ("y2", 3), ("z1", 3), ("z0", 1),
    ("y2", 2), ("d4", "raw"), ("x2a", 1), ("y2", 1), ("z1", 2), ("d1", 3), ("x2b", 3), ("y2", 0),
    ("ay2", "raw"), ("d1", 2), ("z2", 3), ("x2b", 2), ("d1", 1), ("z1", 1), ("x2b", 1), ("d1", 0), ("x2b", 0),
    ("z2", 2), ("d2", 3), ("z3", 3), ("ay1", 3), ("d2", 2), ("x2a", 0), ("z2", 1), ("ay0", 2), ("d2", 1),
    ("d3", "raw"), ("ay1", 2), ("z3", 2), ("ay2", 3), ("d4", 3), ("z3", 1), ("d2", 0), ("d4", 2), ("ay2", 2),
    ("fix", 0), ("d3", 3), ("fix", 1), ("d3", 2), ("d4", 1), ("fix", 2), ("fix", 3),
]


def here():
    r = lax.axis_index("replica")
    f = lax.axis_index("fsdp")
    x = (r // NZ) * 2 + lax.rem(f // 2, 2)
    return x, f // 4, lax.rem(r, NZ), lax.rem(f, 2)


def device(x, y, z, c):
    x = lax.rem(x + NX, NX)
    y = lax.rem(y + NY, NY)
    z = lax.rem(z + NZ, NZ)
    return ((x // 2) * NZ + z, y * 4 + lax.rem(x, 2) * 2 + c)


def block_mask(shape, row_width, column_width):
    rows = lax.broadcasted_iota(jnp.int32, shape, 0) // row_width
    columns = lax.broadcasted_iota(jnp.int32, shape, 1) // column_width
    return rows == columns


def make_bases(kept_ref, forward, inverse):
    lanes = jnp.concatenate([kept_ref[...]] * 4, axis=1)
    freq = jnp.broadcast_to(lanes, (BLOCK, 4 * KEEP))
    place = lax.broadcasted_iota(jnp.int32, (BLOCK, 4 * KEEP), 0)
    turn = ((2 * place + 1) * freq) & (4 * BLOCK - 1)
    angle = turn.astype(jnp.float32) * (jnp.pi / (2 * BLOCK))
    scale = jnp.where(freq == 0, (1.0 / BLOCK) ** 0.5, (2.0 / BLOCK) ** 0.5).astype(jnp.float32)
    basis = scale * jnp.cos(angle)
    wide = jnp.concatenate([basis] * 4, axis=0)
    wide = jnp.where(block_mask(wide.shape, BLOCK, KEEP), wide, 0.0)
    high = wide.astype(jnp.bfloat16)
    forward[:, : 4 * KEEP] = high
    forward[:, 4 * KEEP :] = (wide - high.astype(jnp.float32)).astype(jnp.bfloat16)
    back = jnp.concatenate([basis.T * 0.7] * 4, axis=1)
    back = jnp.where(block_mask(back.shape, KEEP, BLOCK), back, 0.0)
    high = back.astype(jnp.bfloat16)
    inverse[: 4 * KEEP, :] = high
    inverse[4 * KEEP :, :] = (back - high.astype(jnp.float32)).astype(jnp.bfloat16)


def outer_kernel(local_ref, glob_ref, mom_in, kept_ref, T, new_mom,
                 lbuf, gbuf, mom, steps, forward, inverse, lhs, coefs, parts, swap_out, swap_in, means,
                 load_sem, send_sem, recv_sem):
    x, y, z, c = here()
    all_copies = []

    def remote(src, dst, to, landing=None):
        i = len(all_copies)
        copy = pltpu.make_async_remote_copy(
            src, dst, send_sem.at[i], recv_sem.at[i], device_id=to
        )
        copy.start()
        all_copies.append(copy)
        if landing is None:
            return copy
        return pltpu.make_async_remote_copy(
            src, landing, send_sem.at[i], recv_sem.at[i], device_id=to
        )

    flying = {}

    def arrive(*names):
        for name in names:
            for copy in flying.pop(name, []):
                copy.wait_recv()

    sibling = device(x, y, z, 1 - c)
    up, down = device(x, y + 1, z, c), device(x, y - 1, z, c)
    right, left = device(x + 1, y, z, c), device(x - 1, y, z, c)
    far = device(x + 2, y, z, c)
    along = [device(x, y, z + d, c) for d in range(NZ)]
    ahead, behind = along[1], along[NZ - 1]
    barrier = pltpu.get_barrier_semaphore()
    peers = along[1:] + [far, up, down, right, left, sibling]
    for peer in peers:
        pl.semaphore_signal(barrier, inc=1, device_id=peer)

    loads = []
    first = pl.ds(*CHUNKS[0])
    raw_load = pltpu.make_async_copy(
        glob_ref.at[first], T.at[0, 0, first], load_sem.at[2 * NQ + 1]
    )
    raw_load.start()
    for q, (start, size) in enumerate(CHUNKS):
        rows = pl.ds(start, size)
        pair = [
            pltpu.make_async_copy(local_ref.at[0, rows], lbuf.at[rows], load_sem.at[2 * q]),
            pltpu.make_async_copy(glob_ref.at[rows], gbuf.at[rows], load_sem.at[2 * q + 1]),
        ]
        for copy in pair:
            copy.start()
        loads.append(pair)
    mom_load = pltpu.make_async_copy(mom_in, mom, load_sem.at[2 * NQ])
    mom_load.start()
    pl.semaphore_wait(barrier, len(peers))

    def zi(k):
        return lax.rem(z + k + 2 * NZ, NZ)

    def column_group(i):
        return (i % 2) * NZ + i // 2

    ready = []

    def coef(q):
        if not ready:
            make_bases(kept_ref, forward, inverse)
            ready.append(q)
        for copy in loads[q]:
            copy.wait()
        start, size = CHUNKS[q]
        rows = pl.ds(start, size)
        for i in range(GROUPS):
            cols = pl.ds(column_group(i) * GW, GW)
            delta = gbuf[rows, cols].astype(jnp.float32) - lbuf[rows, cols].astype(jnp.float32)
            lhs[pl.ds(i * size, size), :] = delta.astype(jnp.bfloat16)
        both = jnp.dot(
            lhs[: GROUPS * size], forward[...], preferred_element_type=jnp.float32
        )
        out = both[:, : 4 * KEEP] + both[:, 4 * KEEP :]
        coefs[:, :, rows] = out.astype(jnp.bfloat16).reshape(NZ, 2, size, 4 * KEEP)
        return [
            remote(coefs.at[zi(d), :, rows], parts.at[d, :, rows], along[d])
            for d in range(1, NZ)
        ]

    def partial_sum(q):
        arrive(("coef", q))
        rows = pl.ds(*CHUNKS[q])
        total = coefs[z, :, rows].astype(jnp.float32)
        for d in range(1, NZ):
            total = total + parts[d, :, rows].astype(jnp.float32)
        swap_out[:, rows] = total.astype(jnp.bfloat16)
        return [remote(swap_out.at[:, rows], swap_in.at[:, rows], far)]

    def mean(q):
        arrive(("sum", q))
        rows = pl.ds(*CHUNKS[q])
        total = swap_out[:, rows].astype(jnp.float32) + swap_in[:, rows].astype(jnp.float32)
        means[z, :, rows] = (total * (1.0 / REPLICAS)).astype(jnp.bfloat16)
        return [
            remote(means.at[z, :, rows], means.at[z, :, rows], along[d],
                   means.at[zi(-d), :, rows])
            for d in range(1, NZ)
        ]

    def subtract(size, get, put):
        update = jnp.dot(
            lhs[: GROUPS * size, : 8 * KEEP], inverse[...], preferred_element_type=jnp.float32
        )
        for i in range(GROUPS):
            cols = pl.ds(column_group(i) * GW, GW)
            rest = get(cols).astype(jnp.float32) - update[i * size : (i + 1) * size]
            put(cols, rest.astype(jnp.bfloat16))

    def new_rows(q):
        arrive(("mean", q))
        if not mom_ready:
            mom_load.wait()
            mom_ready.append(q)
        start, size = CHUNKS[q]
        rows = pl.ds(start, size)
        for i in range(GROUPS):
            cols = pl.ds(column_group(i) * 4 * KEEP, 4 * KEEP)
            avg = means[i // 2, i % 2, rows].astype(jnp.float32)
            fresh = 0.9 * mom[rows, cols] + avg
            new_mom[rows, cols] = fresh
            step = (avg + 0.9 * fresh).astype(jnp.bfloat16)
            if q == 0:
                steps[0, 0, :, cols] = step
            else:
                lhs[pl.ds(i * size, size), : 4 * KEEP] = step
                lhs[pl.ds(i * size, size), 4 * KEEP : 8 * KEEP] = step

        def put(cols, value):
            T[0, 0, rows, cols] = value

        if q > 0:
            subtract(size, lambda cols: gbuf[rows, cols], put)
        return []

    mom_ready = []

    def load_raw(q):
        raw_load.wait()
        return []

    def finish_raw(part):
        parity = part // 2
        if part == 0:
            arrive(*[key for key in flying if key[1] in ("raw", 0) and key[0] not in SHARES])
            for copy in raw_copies:
                copy.wait_send()
        if part == 2:
            arrive(*[key for key in flying if key[1] in ("raw", 0)])
        size = CHUNKS[0][1]

        def one(n, carry):
            slot = (part % 2) * 4 + n
            for i in range(GROUPS):
                cols = pl.ds(column_group(i) * 4 * KEEP, 4 * KEEP)
                step = steps[parity, slot, :, cols]
                lhs[pl.ds(i * size, size), : 4 * KEEP] = step
                lhs[pl.ds(i * size, size), 4 * KEEP : 8 * KEEP] = step

            def put(cols, value):
                T[parity, slot, first, cols] = value

            subtract(size, lambda cols: T[parity, slot, first, cols], put)
            return carry

        lax.fori_loop(0, 4, one, 0)
        return []

    def pass_on(q, name):
        a1, a2, b = SPLIT[q]
        a = a1 + a2
        width = a + NZ * b
        buf = steps if q == 0 else T
        rows = pl.ds(0, CHUNKS[0][1]) if q == 0 else first if q == "raw" else pl.ds(*CHUNKS[q])
        odd = 0 if q == "raw" else q % 2
        p, p0, p1 = pl.ds(0, a1), pl.ds(0, a1 // 2), pl.ds(a1 // 2, a1 // 2)
        s, s0, s1 = pl.ds(a1, a2), pl.ds(a1, a2 // 2), pl.ds(a1 + a2 // 2, a2 // 2)

        def strip(k):
            return pl.ds(pl.multiple_of(a + zi(k) * b, 128), b)

        def send(slot, to_slot, cols, to, landing=None):
            return remote(
                buf.at[0, slot, rows, cols], buf.at[0, to_slot, rows, cols], to,
                None if landing is None else buf.at[0, to_slot, rows, landing],
            )

        def share(slot, cols):
            return [remote(buf.at[0, slot, rows, cols], buf.at[1, slot, rows, cols], sibling)]

        near, away = pl.ds(1, 3), pl.ds(5, 3)
        others = pl.ds(1, 7)
        if name == "ox1":
            return [send(0, 4, p0, right), send(0, 4, p1, left)]
        if name == "oy":
            return [send(0, 3, p, up), send(0, 1, p, down)]
        if name == "od":
            return share(0, pl.ds(0, width))
        if name == "y2":
            arrive(("oy", q))
            return [send(3, 2, p0, up), send(1, 2, p1, down)]
        if name == "x2a":
            arrive(("oy", q))
            return [send(i, i + 4, h, to) for i in (1, 3) for h, to in ((p0, right), (p1, left))]
        if name == "x2b":
            arrive(("y2", q))
            return [send(2, 6, p0, right), send(2, 6, p1, left)]
        if name == "d1":
            arrive(("oy", q), ("y2", q))
            return share(near, p)
        if name == "d2":
            arrive(("ox1", q), ("x2a", q), ("x2b", q))
            return share(pl.ds(4, 4), p)
        if name == "ox2":
            return [send(0, 4, s0, right), send(0, 4, s1, left)]
        if name == "ay0":
            return [send(0, 3, s, up), send(0, 1, s, down)]
        if name == "ay1":
            arrive(("ox2", q))
            return [send(4, 7, s, up), send(4, 5, s, down)]
        if name == "ay2":
            arrive(("ay0", q), ("ay1", q))
            return [send(3, 2, s, up), send(5, 6, s, down)]
        if name == "d3":
            arrive(("ay2", q))
            return share(others, s)
        mine = strip(0)
        if name == "oyB":
            return [send(0, 3, mine, up), send(0, 1, mine, down)]
        if name == "oxB":
            return [send(0, 4, mine, right if odd else left)]
        if name == "yB2":
            arrive(("oyB", q))
            return [send(1, 2, mine, down) if odd else send(3, 2, mine, up)]
        if name == "xB2":
            arrive(("yB2", q))
            return [send(near, away, mine, left if odd else right)]
        if name == "d4":
            arrive(("z3", q))
            return share(others, pl.ds(a, width - a))
        hop = int(name[1])
        arrive(*((("xB2", q), ("oxB", q)) if hop == 0 else (("z%d" % (hop - 1), q),)))
        onward = [
            (strip(-hop), ahead, strip(-hop - 1)),
            (strip(hop), behind, strip(hop + 1)),
        ]
        if hop == 3:
            onward = onward[odd : odd + 1]
        return [send(others, others, cols, to, landing) for cols, to, landing in onward]

    raw_copies = []
    compute = {"coef": coef, "sum": partial_sum, "mean": mean, "rows": new_rows,
               "load": load_raw, "fix": finish_raw}
    for name, q in ORDER:
        before = len(all_copies)
        if name in compute:
            flying[name, q] = compute[name](q)
        else:
            flying[name, q] = pass_on(q, name)
        if q == "raw":
            raw_copies += all_copies[before:]
    arrive(*list(flying))
    for copy in all_copies:
        if not any(copy is other for other in raw_copies):
            copy.wait_send()


def place_kernel(T, mom, params, new_mom, sem):
    x, y, z, c = here()
    copies = [pltpu.make_async_copy(mom, new_mom, sem.at[16])]
    for p in range(2):
        for dy in range(4):
            for dx in range(2):
                slot = dx * 4 + dy
                shard = (
                    lax.rem(y + dy, NY) * 4 + lax.rem(x + dx, 2) * 2 + lax.rem(c + p, 2)
                )
                rows = pl.ds(pl.multiple_of(shard * SHARD, SHARD), SHARD)
                copies.append(
                    pltpu.make_async_copy(
                        T.at[p, slot], params.at[rows], sem.at[p * 8 + slot]
                    )
                )
    for copy in copies:
        copy.start()
    for copy in copies:
        copy.wait()


def on_device(local_params, global_params, momentum, kept):
    lanes = kept[None, :]
    bf16, f32 = jnp.bfloat16, jnp.float32
    anywhere = pl.BlockSpec(memory_space=pl.ANY)
    in_vmem = pl.BlockSpec(memory_space=pltpu.VMEM)
    T, mom = pl.pallas_call(
        outer_kernel,
        out_shape=(pltpu.VMEM((2, 8, SHARD, D), bf16), pltpu.VMEM((SHARD, D // 4), f32)),
        in_specs=[anywhere, anywhere, anywhere, in_vmem],
        out_specs=(in_vmem, in_vmem),
        scratch_shapes=[
            pltpu.VMEM((SHARD, D), bf16),
            pltpu.VMEM((SHARD, D), bf16),
            pltpu.VMEM((SHARD, D // 4), f32),
            pltpu.VMEM((2, 8, CHUNKS[0][1], D // 4), bf16),
            pltpu.VMEM((GW, 8 * KEEP), bf16),
            pltpu.VMEM((8 * KEEP, GW), bf16),
            pltpu.VMEM((GROUPS * max(size for _, size in CHUNKS), GW), bf16),
            pltpu.VMEM((NZ, 2, SHARD, 4 * KEEP), bf16),
            pltpu.VMEM((NZ, 2, SHARD, 4 * KEEP), bf16),
            pltpu.VMEM((2, SHARD, 4 * KEEP), bf16),
            pltpu.VMEM((2, SHARD, 4 * KEEP), bf16),
            pltpu.VMEM((NZ, 2, SHARD, 4 * KEEP), bf16),
            pltpu.SemaphoreType.DMA((2 * NQ + 2,)),
            pltpu.SemaphoreType.DMA((SEMAPHORES,)),
            pltpu.SemaphoreType.DMA((SEMAPHORES,)),
        ],
        compiler_params=pltpu.CompilerParams(
            collective_id=0, has_side_effects=True, vmem_limit_bytes=VMEM
        ),
    )(local_params, global_params, momentum, lanes)
    return pl.pallas_call(
        place_kernel,
        out_shape=(
            jax.ShapeDtypeStruct((ROWS, D), bf16),
            jax.ShapeDtypeStruct((SHARD, D // 4), f32),
        ),
        in_specs=[in_vmem, in_vmem],
        out_specs=(anywhere, anywhere),
        scratch_shapes=[pltpu.SemaphoreType.DMA((17,))],
        compiler_params=pltpu.CompilerParams(vmem_limit_bytes=VMEM),
    )(
        pltpu.with_memory_space_constraint(T, pltpu.VMEM),
        pltpu.with_memory_space_constraint(mom, pltpu.VMEM),
    )


def solution(mesh):
    in_specs = (P("replica", "fsdp", None), P("fsdp", None), P("fsdp", None), P())
    out_specs = (P(), P("fsdp", None))
    return jax.shard_map(
        on_device, mesh=mesh, in_specs=in_specs, out_specs=out_specs, check_vma=False
    )
```

```python
import jax
import jax.numpy as jnp
from jax import lax
from jax.experimental import pallas as pl
from jax.experimental.pallas import tpu as pltpu
from jax.sharding import PartitionSpec as P

D = 8192
BLOCK = 128
KEEP = 32
ROWS = 2048
SHARD = 128
NZ, NY, NX = 8, 4, 4
REPLICAS = 16
GROUPS = 16
GW = D // GROUPS
VMEM = 24 << 20
CHUNKS = [(0, 48), (48, 16), (64, 32), (96, 32)]
NQ = len(CHUNKS)
SPLIT = {0: (2048, 0, 0), 1: (5120, 0, 384), 2: (4608, 1536, 256), 3: (3840, 1280, 384), 'raw': (2560, 3584, 256)}
SHARES = ("od", "d1", "d2", "d3", "d4")
SEMAPHORES = 214
ORDER = [
    ("load", "raw"), ("ox1", "raw"), ("oyB", "raw"), ("od", "raw"), ("oxB", "raw"), ("ay0", "raw"),
    ("ox2", "raw"), ("coef", 3), ("coef", 2), ("yB2", "raw"), ("coef", 1), ("coef", 0), ("oy", "raw"),
    ("sum", 3), ("xB2", "raw"), ("sum", 2), ("ay1", "raw"), ("sum", 1), ("mean", 3), ("z0", "raw"),
    ("x2a", "raw"), ("mean", 2), ("sum", 0), ("mean", 1), ("y2", "raw"), ("rows", 3), ("ox1", 3), ("oyB", 3),
    ("od", 3), ("oxB", 3), ("ox2", 3), ("ay0", 3), ("oy", 3), ("z1", "raw"), ("d1", "raw"), ("x2b", "raw"),
    ("mean", 0), ("yB2", 3), ("rows", 2), ("ox1", 2), ("oyB", 2), ("od", 2), ("oxB", 2), ("ox2", 2),
    ("rows", 1), ("oyB", 1), ("od", 1), ("oxB", 1), ("oy", 2), ("z2", "raw"), ("d2", "raw"), ("ox1", 1),
    ("xB2", 3), ("yB2", 2), ("yB2", 1), ("x2a", 3), ("oy", 1), ("rows", 0), ("od", 0), ("z0", 3), ("z3", "raw"),
    ("oy", 0), ("xB2", 1), ("xB2", 2), ("ox1", 0), ("x2a", 2), ("z0", 2), ("y2", 3), ("z1", 3), ("z0", 1),
    ("y2", 2), ("d4", "raw"), ("x2a", 1), ("y2", 1), ("z1", 2), ("d1", 3), ("x2b", 3), ("y2", 0),
    ("ay2", "raw"), ("d1", 2), ("z2", 3), ("x2b", 2), ("d1", 1), ("z1", 1), ("x2b", 1), ("d1", 0), ("x2b", 0),
    ("z2", 2), ("d2", 3), ("z3", 3), ("ay1", 3), ("d2", 2), ("x2a", 0), ("z2", 1), ("ay0", 2), ("d2", 1),
    ("d3", "raw"), ("ay1", 2), ("z3", 2), ("ay2", 3), ("d4", 3), ("z3", 1), ("d2", 0), ("d4", 2), ("ay2", 2),
    ("fix", 0), ("d3", 3), ("fix", 1), ("d3", 2), ("d4", 1), ("fix", 2), ("fix", 3),
]


def here():
    r = lax.axis_index("replica")
    f = lax.axis_index("fsdp")
    x = (r // NZ) * 2 + lax.rem(f // 2, 2)
    return x, f // 4, lax.rem(r, NZ), lax.rem(f, 2)


def device(x, y, z, c):
    x = lax.rem(x + NX, NX)
    y = lax.rem(y + NY, NY)
    z = lax.rem(z + NZ, NZ)
    return ((x // 2) * NZ + z, y * 4 + lax.rem(x, 2) * 2 + c)


def block_mask(shape, row_width, column_width):
    rows = lax.broadcasted_iota(jnp.int32, shape, 0) // row_width
    columns = lax.broadcasted_iota(jnp.int32, shape, 1) // column_width
    return rows == columns


def make_bases(kept_ref, forward, inverse):
    lanes = jnp.concatenate([kept_ref[...]] * 4, axis=1)
    freq = jnp.broadcast_to(lanes, (BLOCK, 4 * KEEP))
    place = lax.broadcasted_iota(jnp.int32, (BLOCK, 4 * KEEP), 0)
    turn = ((2 * place + 1) * freq) & (4 * BLOCK - 1)
    angle = turn.astype(jnp.float32) * (jnp.pi / (2 * BLOCK))
    scale = jnp.where(freq == 0, (1.0 / BLOCK) ** 0.5, (2.0 / BLOCK) ** 0.5).astype(jnp.float32)
    basis = scale * jnp.cos(angle)
    wide = jnp.concatenate([basis] * 4, axis=0)
    wide = jnp.where(block_mask(wide.shape, BLOCK, KEEP), wide, 0.0)
    high = wide.astype(jnp.bfloat16)
    forward[:, : 4 * KEEP] = high
    forward[:, 4 * KEEP :] = (wide - high.astype(jnp.float32)).astype(jnp.bfloat16)
    back = jnp.concatenate([basis.T * 0.7] * 4, axis=1)
    back = jnp.where(block_mask(back.shape, KEEP, BLOCK), back, 0.0)
    high = back.astype(jnp.bfloat16)
    inverse[: 4 * KEEP, :] = high
    inverse[4 * KEEP :, :] = (back - high.astype(jnp.float32)).astype(jnp.bfloat16)


def outer_kernel(local_ref, glob_ref, mom_in, kept_ref, T, new_mom,
                 lbuf, gbuf, mom, steps, forward, inverse, lhs, coefs, parts, swap_out, swap_in, means,
                 load_sem, send_sem, recv_sem):
    x, y, z, c = here()
    all_copies = []

    def remote(src, dst, to, landing=None):
        i = len(all_copies)
        copy = pltpu.make_async_remote_copy(
            src, dst, send_sem.at[i], recv_sem.at[i], device_id=to
        )
        copy.start()
        all_copies.append(copy)
        if landing is None:
            return copy
        return pltpu.make_async_remote_copy(
            src, landing, send_sem.at[i], recv_sem.at[i], device_id=to
        )

    flying = {}

    def arrive(*names):
        for name in names:
            for copy in flying.pop(name, []):
                copy.wait_recv()

    sibling = device(x, y, z, 1 - c)
    up, down = device(x, y + 1, z, c), device(x, y - 1, z, c)
    right, left = device(x + 1, y, z, c), device(x - 1, y, z, c)
    far = device(x + 2, y, z, c)
    along = [device(x, y, z + d, c) for d in range(NZ)]
    ahead, behind = along[1], along[NZ - 1]
    barrier = pltpu.get_barrier_semaphore()
    peers = along[1:] + [far, up, down, right, left, sibling]
    for peer in peers:
        pl.semaphore_signal(barrier, inc=1, device_id=peer)

    loads = []
    first = pl.ds(*CHUNKS[0])
    raw_load = pltpu.make_async_copy(
        glob_ref.at[first], T.at[0, 0, first], load_sem.at[2 * NQ + 1]
    )
    raw_load.start()
    for q, (start, size) in enumerate(CHUNKS):
        rows = pl.ds(start, size)
        pair = [
            pltpu.make_async_copy(local_ref.at[0, rows], lbuf.at[rows], load_sem.at[2 * q]),
            pltpu.make_async_copy(glob_ref.at[rows], gbuf.at[rows], load_sem.at[2 * q + 1]),
        ]
        for copy in pair:
            copy.start()
        loads.append(pair)
    mom_load = pltpu.make_async_copy(mom_in, mom, load_sem.at[2 * NQ])
    mom_load.start()
    make_bases(kept_ref, forward, inverse)
    pl.semaphore_wait(barrier, len(peers))

    def zi(k):
        return lax.rem(z + k + 2 * NZ, NZ)

    def column_group(i):
        return (i % 2) * NZ + i // 2

    def coef(q):
        for copy in loads[q]:
            copy.wait()
        start, size = CHUNKS[q]
        rows = pl.ds(start, size)
        for i in range(GROUPS):
            cols = pl.ds(column_group(i) * GW, GW)
            delta = gbuf[rows, cols].astype(jnp.float32) - lbuf[rows, cols].astype(jnp.float32)
            lhs[pl.ds(i * size, size), :] = delta.astype(jnp.bfloat16)
        both = jnp.dot(
            lhs[: GROUPS * size], forward[...], preferred_element_type=jnp.float32
        )
        out = both[:, : 4 * KEEP] + both[:, 4 * KEEP :]
        coefs[:, :, rows] = out.astype(jnp.bfloat16).reshape(NZ, 2, size, 4 * KEEP)
        return [
            remote(coefs.at[zi(d), :, rows], parts.at[d, :, rows], along[d])
            for d in range(1, NZ)
        ]

    def partial_sum(q):
        arrive(("coef", q))
        rows = pl.ds(*CHUNKS[q])
        total = coefs[z, :, rows].astype(jnp.float32)
        for d in range(1, NZ):
            total = total + parts[d, :, rows].astype(jnp.float32)
        swap_out[:, rows] = total.astype(jnp.bfloat16)
        return [remote(swap_out.at[:, rows], swap_in.at[:, rows], far)]

    def mean(q):
        arrive(("sum", q))
        rows = pl.ds(*CHUNKS[q])
        total = swap_out[:, rows].astype(jnp.float32) + swap_in[:, rows].astype(jnp.float32)
        means[z, :, rows] = (total * (1.0 / REPLICAS)).astype(jnp.bfloat16)
        return [
            remote(means.at[z, :, rows], means.at[z, :, rows], along[d],
                   means.at[zi(-d), :, rows])
            for d in range(1, NZ)
        ]

    def subtract(size, get, put):
        update = jnp.dot(
            lhs[: GROUPS * size, : 8 * KEEP], inverse[...], preferred_element_type=jnp.float32
        )
        for i in range(GROUPS):
            cols = pl.ds(column_group(i) * GW, GW)
            rest = get(cols).astype(jnp.float32) - update[i * size : (i + 1) * size]
            put(cols, rest.astype(jnp.bfloat16))

    def new_rows(q):
        arrive(("mean", q))
        if not mom_ready:
            mom_load.wait()
            mom_ready.append(q)
        start, size = CHUNKS[q]
        rows = pl.ds(start, size)
        for i in range(GROUPS):
            cols = pl.ds(column_group(i) * 4 * KEEP, 4 * KEEP)
            avg = means[i // 2, i % 2, rows].astype(jnp.float32)
            fresh = 0.9 * mom[rows, cols] + avg
            new_mom[rows, cols] = fresh
            step = (avg + 0.9 * fresh).astype(jnp.bfloat16)
            if q == 0:
                steps[0, 0, :, cols] = step
            else:
                lhs[pl.ds(i * size, size), : 4 * KEEP] = step
                lhs[pl.ds(i * size, size), 4 * KEEP : 8 * KEEP] = step

        def put(cols, value):
            T[0, 0, rows, cols] = value

        if q > 0:
            subtract(size, lambda cols: gbuf[rows, cols], put)
        return []

    mom_ready = []

    def load_raw(q):
        raw_load.wait()
        return []

    def finish_raw(part):
        parity = part // 2
        if part == 0:
            arrive(*[key for key in flying if key[1] in ("raw", 0) and key[0] not in SHARES])
            for copy in raw_copies:
                copy.wait_send()
        if part == 2:
            arrive(*[key for key in flying if key[1] in ("raw", 0)])
        size = CHUNKS[0][1]

        def one(n, carry):
            slot = (part % 2) * 4 + n
            for i in range(GROUPS):
                cols = pl.ds(column_group(i) * 4 * KEEP, 4 * KEEP)
                step = steps[parity, slot, :, cols]
                lhs[pl.ds(i * size, size), : 4 * KEEP] = step
                lhs[pl.ds(i * size, size), 4 * KEEP : 8 * KEEP] = step

            def put(cols, value):
                T[parity, slot, first, cols] = value

            subtract(size, lambda cols: T[parity, slot, first, cols], put)
            return carry

        lax.fori_loop(0, 4, one, 0)
        return []

    def pass_on(q, name):
        a1, a2, b = SPLIT[q]
        a = a1 + a2
        width = a + NZ * b
        buf = steps if q == 0 else T
        rows = pl.ds(0, CHUNKS[0][1]) if q == 0 else first if q == "raw" else pl.ds(*CHUNKS[q])
        odd = 0 if q == "raw" else q % 2
        p, p0, p1 = pl.ds(0, a1), pl.ds(0, a1 // 2), pl.ds(a1 // 2, a1 // 2)
        s, s0, s1 = pl.ds(a1, a2), pl.ds(a1, a2 // 2), pl.ds(a1 + a2 // 2, a2 // 2)

        def strip(k):
            return pl.ds(pl.multiple_of(a + zi(k) * b, 128), b)

        def send(slot, to_slot, cols, to, landing=None):
            return remote(
                buf.at[0, slot, rows, cols], buf.at[0, to_slot, rows, cols], to,
                None if landing is None else buf.at[0, to_slot, rows, landing],
            )

        def share(slot, cols):
            return [remote(buf.at[0, slot, rows, cols], buf.at[1, slot, rows, cols], sibling)]

        near, away = pl.ds(1, 3), pl.ds(5, 3)
        others = pl.ds(1, 7)
        if name == "ox1":
            return [send(0, 4, p0, right), send(0, 4, p1, left)]
        if name == "oy":
            return [send(0, 3, p, up), send(0, 1, p, down)]
        if name == "od":
            return share(0, pl.ds(0, width))
        if name == "y2":
            arrive(("oy", q))
            return [send(3, 2, p0, up), send(1, 2, p1, down)]
        if name == "x2a":
            arrive(("oy", q))
            return [send(i, i + 4, h, to) for i in (1, 3) for h, to in ((p0, right), (p1, left))]
        if name == "x2b":
            arrive(("y2", q))
            return [send(2, 6, p0, right), send(2, 6, p1, left)]
        if name == "d1":
            arrive(("oy", q), ("y2", q))
            return share(near, p)
        if name == "d2":
            arrive(("ox1", q), ("x2a", q), ("x2b", q))
            return share(pl.ds(4, 4), p)
        if name == "ox2":
            return [send(0, 4, s0, right), send(0, 4, s1, left)]
        if name == "ay0":
            return [send(0, 3, s, up), send(0, 1, s, down)]
        if name == "ay1":
            arrive(("ox2", q))
            return [send(4, 7, s, up), send(4, 5, s, down)]
        if name == "ay2":
            arrive(("ay0", q), ("ay1", q))
            return [send(3, 2, s, up), send(5, 6, s, down)]
        if name == "d3":
            arrive(("ay2", q))
            return share(others, s)
        mine = strip(0)
        if name == "oyB":
            return [send(0, 3, mine, up), send(0, 1, mine, down)]
        if name == "oxB":
            return [send(0, 4, mine, right if odd else left)]
        if name == "yB2":
            arrive(("oyB", q))
            return [send(1, 2, mine, down) if odd else send(3, 2, mine, up)]
        if name == "xB2":
            arrive(("yB2", q))
            return [send(near, away, mine, left if odd else right)]
        if name == "d4":
            arrive(("z3", q))
            return share(others, pl.ds(a, width - a))
        hop = int(name[1])
        arrive(*((("xB2", q), ("oxB", q)) if hop == 0 else (("z%d" % (hop - 1), q),)))
        onward = [
            (strip(-hop), ahead, strip(-hop - 1)),
            (strip(hop), behind, strip(hop + 1)),
        ]
        if hop == 3:
            onward = onward[odd : odd + 1]
        return [send(others, others, cols, to, landing) for cols, to, landing in onward]

    raw_copies = []
    compute = {"coef": coef, "sum": partial_sum, "mean": mean, "rows": new_rows,
               "load": load_raw, "fix": finish_raw}
    for name, q in ORDER:
        before = len(all_copies)
        if name in compute:
            flying[name, q] = compute[name](q)
        else:
            flying[name, q] = pass_on(q, name)
        if q == "raw":
            raw_copies += all_copies[before:]
    arrive(*list(flying))
    for copy in all_copies:
        if not any(copy is other for other in raw_copies):
            copy.wait_send()


def place_kernel(T, mom, params, new_mom, sem):
    x, y, z, c = here()
    copies = [pltpu.make_async_copy(mom, new_mom, sem.at[16])]
    for p in range(2):
        for dy in range(4):
            for dx in range(2):
                slot = dx * 4 + dy
                shard = (
                    lax.rem(y + dy, NY) * 4 + lax.rem(x + dx, 2) * 2 + lax.rem(c + p, 2)
                )
                rows = pl.ds(pl.multiple_of(shard * SHARD, SHARD), SHARD)
                copies.append(
                    pltpu.make_async_copy(
                        T.at[p, slot], params.at[rows], sem.at[p * 8 + slot]
                    )
                )
    for copy in copies:
        copy.start()
    for copy in copies:
        copy.wait()


def on_device(local_params, global_params, momentum, kept):
    lanes = kept[None, :]
    bf16, f32 = jnp.bfloat16, jnp.float32
    anywhere = pl.BlockSpec(memory_space=pl.ANY)
    in_vmem = pl.BlockSpec(memory_space=pltpu.VMEM)
    T, mom = pl.pallas_call(
        outer_kernel,
        out_shape=(pltpu.VMEM((2, 8, SHARD, D), bf16), pltpu.VMEM((SHARD, D // 4), f32)),
        in_specs=[anywhere, anywhere, anywhere, in_vmem],
        out_specs=(in_vmem, in_vmem),
        scratch_shapes=[
            pltpu.VMEM((SHARD, D), bf16),
            pltpu.VMEM((SHARD, D), bf16),
            pltpu.VMEM((SHARD, D // 4), f32),
            pltpu.VMEM((2, 8, CHUNKS[0][1], D // 4), bf16),
            pltpu.VMEM((GW, 8 * KEEP), bf16),
            pltpu.VMEM((8 * KEEP, GW), bf16),
            pltpu.VMEM((GROUPS * max(size for _, size in CHUNKS), GW), bf16),
            pltpu.VMEM((NZ, 2, SHARD, 4 * KEEP), bf16),
            pltpu.VMEM((NZ, 2, SHARD, 4 * KEEP), bf16),
            pltpu.VMEM((2, SHARD, 4 * KEEP), bf16),
            pltpu.VMEM((2, SHARD, 4 * KEEP), bf16),
            pltpu.VMEM((NZ, 2, SHARD, 4 * KEEP), bf16),
            pltpu.SemaphoreType.DMA((2 * NQ + 2,)),
            pltpu.SemaphoreType.DMA((SEMAPHORES,)),
            pltpu.SemaphoreType.DMA((SEMAPHORES,)),
        ],
        compiler_params=pltpu.CompilerParams(
            collective_id=0, has_side_effects=True, vmem_limit_bytes=VMEM
        ),
    )(local_params, global_params, momentum, lanes)
    return pl.pallas_call(
        place_kernel,
        out_shape=(
            jax.ShapeDtypeStruct((ROWS, D), bf16),
            jax.ShapeDtypeStruct((SHARD, D // 4), f32),
        ),
        in_specs=[in_vmem, in_vmem],
        out_specs=(anywhere, anywhere),
        scratch_shapes=[pltpu.SemaphoreType.DMA((17,))],
        compiler_params=pltpu.CompilerParams(vmem_limit_bytes=VMEM),
    )(
        pltpu.with_memory_space_constraint(T, pltpu.VMEM),
        pltpu.with_memory_space_constraint(mom, pltpu.VMEM),
    )


def solution(mesh):
    in_specs = (P("replica", "fsdp", None), P("fsdp", None), P("fsdp", None), P())
    out_specs = (P(), P("fsdp", None))
    return jax.shard_map(
        on_device, mesh=mesh, in_specs=in_specs, out_specs=out_specs, check_vma=False
    )
```

```python
import jax
import jax.numpy as jnp
from jax import lax
from jax.experimental import pallas as pl
from jax.experimental.pallas import tpu as pltpu
from jax.sharding import PartitionSpec as P

D = 8192
BLOCK = 128
KEEP = 32
ROWS = 2048
SHARD = 128
NZ, NY, NX = 8, 4, 4
REPLICAS = 16
GROUPS = 16
GW = D // GROUPS
PIECES = 4
VMEM = 24 << 20
CHUNKS = [(0, 48), (48, 16), (64, 32), (96, 32)]
NQ = len(CHUNKS)
SPLIT = {0: (2048, 0, 0), 1: (5120, 0, 384), 2: (4608, 1536, 256), 3: (3840, 1280, 384), 'raw': (2560, 3584, 256)}
SHARES = ("od", "d1", "d2", "d3", "d4")
SEMAPHORES = 214
ORDER = [
    ("load", "raw"), ("ox1", "raw"), ("oyB", "raw"), ("od", "raw"), ("oxB", "raw"), ("ay0", "raw"),
    ("ox2", "raw"), ("coef", 3), ("coef", 2), ("yB2", "raw"), ("coef", 1), ("coef", 0), ("oy", "raw"),
    ("sum", 3), ("xB2", "raw"), ("sum", 2), ("ay1", "raw"), ("sum", 1), ("mean", 3), ("z0", "raw"),
    ("x2a", "raw"), ("mean", 2), ("sum", 0), ("mean", 1), ("y2", "raw"), ("rows", 3), ("ox1", 3), ("oyB", 3),
    ("od", 3), ("oxB", 3), ("ox2", 3), ("ay0", 3), ("oy", 3), ("z1", "raw"), ("d1", "raw"), ("x2b", "raw"),
    ("mean", 0), ("yB2", 3), ("rows", 2), ("ox1", 2), ("oyB", 2), ("od", 2), ("oxB", 2), ("ox2", 2),
    ("rows", 1), ("oyB", 1), ("od", 1), ("oxB", 1), ("oy", 2), ("z2", "raw"), ("d2", "raw"), ("ox1", 1),
    ("xB2", 3), ("yB2", 2), ("yB2", 1), ("x2a", 3), ("oy", 1), ("rows", 0), ("od", 0), ("z0", 3), ("z3", "raw"),
    ("oy", 0), ("xB2", 1), ("xB2", 2), ("ox1", 0), ("x2a", 2), ("z0", 2), ("y2", 3), ("z1", 3), ("z0", 1),
    ("y2", 2), ("d4", "raw"), ("x2a", 1), ("y2", 1), ("z1", 2), ("d1", 3), ("x2b", 3), ("y2", 0),
    ("ay2", "raw"), ("d1", 2), ("z2", 3), ("x2b", 2), ("d1", 1), ("z1", 1), ("x2b", 1), ("d1", 0), ("x2b", 0),
    ("z2", 2), ("d2", 3), ("z3", 3), ("ay1", 3), ("d2", 2), ("x2a", 0), ("z2", 1), ("ay0", 2), ("d2", 1),
    ("d3", "raw"), ("ay1", 2), ("z3", 2), ("ay2", 3), ("d4", 3), ("z3", 1), ("d2", 0), ("d4", 2), ("ay2", 2),
    ("fix", 0), ("d3", 3), ("fix", 1), ("d3", 2), ("d4", 1), ("fix", 2), ("fix", 3),
]


def here():
    r = lax.axis_index("replica")
    f = lax.axis_index("fsdp")
    x = (r // NZ) * 2 + lax.rem(f // 2, 2)
    return x, f // 4, lax.rem(r, NZ), lax.rem(f, 2)


def device(x, y, z, c):
    x = lax.rem(x + NX, NX)
    y = lax.rem(y + NY, NY)
    z = lax.rem(z + NZ, NZ)
    return ((x // 2) * NZ + z, y * 4 + lax.rem(x, 2) * 2 + c)


def block_mask(shape, row_width, column_width):
    rows = lax.broadcasted_iota(jnp.int32, shape, 0) // row_width
    columns = lax.broadcasted_iota(jnp.int32, shape, 1) // column_width
    return rows == columns


def make_bases(kept_ref, forward, inverse):
    lanes = jnp.concatenate([kept_ref[...]] * 4, axis=1)
    freq = jnp.broadcast_to(lanes, (BLOCK, 4 * KEEP))
    place = lax.broadcasted_iota(jnp.int32, (BLOCK, 4 * KEEP), 0)
    turn = ((2 * place + 1) * freq) & (4 * BLOCK - 1)
    angle = turn.astype(jnp.float32) * (jnp.pi / (2 * BLOCK))
    scale = jnp.where(freq == 0, (1.0 / BLOCK) ** 0.5, (2.0 / BLOCK) ** 0.5).astype(jnp.float32)
    basis = scale * jnp.cos(angle)
    wide = jnp.concatenate([basis] * 4, axis=0)
    wide = jnp.where(block_mask(wide.shape, BLOCK, KEEP), wide, 0.0)
    high = wide.astype(jnp.bfloat16)
    forward[:, : 4 * KEEP] = high
    forward[:, 4 * KEEP :] = (wide - high.astype(jnp.float32)).astype(jnp.bfloat16)
    back = jnp.concatenate([basis.T * 0.7] * 4, axis=1)
    back = jnp.where(block_mask(back.shape, KEEP, BLOCK), back, 0.0)
    high = back.astype(jnp.bfloat16)
    inverse[: 4 * KEEP, :] = high
    inverse[4 * KEEP :, :] = (back - high.astype(jnp.float32)).astype(jnp.bfloat16)


def outer_kernel(local_ref, glob_ref, mom_in, kept_ref, T, new_mom,
                 lbuf, gbuf, mom, steps, forward, inverse, lhs, coefs, parts, swap_out, swap_in, means,
                 load_sem, send_sem, recv_sem):
    x, y, z, c = here()
    all_copies = []

    def remote(src, dst, to, landing=None):
        i = len(all_copies)
        copy = pltpu.make_async_remote_copy(
            src, dst, send_sem.at[i], recv_sem.at[i], device_id=to
        )
        copy.start()
        all_copies.append(copy)
        if landing is None:
            return copy
        return pltpu.make_async_remote_copy(
            src, landing, send_sem.at[i], recv_sem.at[i], device_id=to
        )

    flying = {}

    def arrive(*names):
        for name in names:
            for copy in flying.pop(name, []):
                copy.wait_recv()

    sibling = device(x, y, z, 1 - c)
    up, down = device(x, y + 1, z, c), device(x, y - 1, z, c)
    right, left = device(x + 1, y, z, c), device(x - 1, y, z, c)
    far = device(x + 2, y, z, c)
    along = [device(x, y, z + d, c) for d in range(NZ)]
    ahead, behind = along[1], along[NZ - 1]
    barrier = pltpu.get_barrier_semaphore()
    peers = along[1:] + [far, up, down, right, left, sibling]
    for peer in peers:
        pl.semaphore_signal(barrier, inc=1, device_id=peer)

    loads = []
    first = pl.ds(*CHUNKS[0])
    raw_load = pltpu.make_async_copy(
        glob_ref.at[first], T.at[0, 0, first], load_sem.at[2 * NQ + 1]
    )
    raw_load.start()
    for q, (start, size) in enumerate(CHUNKS):
        rows = pl.ds(start, size)
        pair = [
            pltpu.make_async_copy(local_ref.at[0, rows], lbuf.at[rows], load_sem.at[2 * q]),
            pltpu.make_async_copy(glob_ref.at[rows], gbuf.at[rows], load_sem.at[2 * q + 1]),
        ]
        for copy in pair:
            copy.start()
        loads.append(pair)
    mom_load = pltpu.make_async_copy(mom_in, mom, load_sem.at[2 * NQ])
    mom_load.start()
    make_bases(kept_ref, forward, inverse)
    pl.semaphore_wait(barrier, len(peers))

    def zi(k):
        return lax.rem(z + k + 2 * NZ, NZ)

    def column_group(i):
        return (i % 2) * NZ + i // 2

    def coef(q):
        for copy in loads[q]:
            copy.wait()
        start, size = CHUNKS[q]
        rows = pl.ds(start, size)
        for i in range(GROUPS):
            cols = pl.ds(column_group(i) * GW, GW)
            delta = gbuf[rows, cols].astype(jnp.float32) - lbuf[rows, cols].astype(jnp.float32)
            lhs[pl.ds(i * size, size), :] = delta.astype(jnp.bfloat16)
        both = jnp.dot(
            lhs[: GROUPS * size], forward[...], preferred_element_type=jnp.float32
        )
        out = both[:, : 4 * KEEP] + both[:, 4 * KEEP :]
        coefs[:, :, rows] = out.astype(jnp.bfloat16).reshape(NZ, 2, size, 4 * KEEP)
        return [
            remote(coefs.at[zi(d), :, rows], parts.at[d, :, rows], along[d])
            for d in range(1, NZ)
        ]

    def partial_sum(q):
        arrive(("coef", q))
        rows = pl.ds(*CHUNKS[q])
        total = coefs[z, :, rows].astype(jnp.float32)
        for d in range(1, NZ):
            total = total + parts[d, :, rows].astype(jnp.float32)
        swap_out[:, rows] = total.astype(jnp.bfloat16)
        return [remote(swap_out.at[:, rows], swap_in.at[:, rows], far)]

    def mean(q):
        arrive(("sum", q))
        rows = pl.ds(*CHUNKS[q])
        total = swap_out[:, rows].astype(jnp.float32) + swap_in[:, rows].astype(jnp.float32)
        means[z, :, rows] = (total * (1.0 / REPLICAS)).astype(jnp.bfloat16)
        return [
            remote(means.at[z, :, rows], means.at[z, :, rows], along[d],
                   means.at[zi(-d), :, rows])
            for d in range(1, NZ)
        ]

    def subtract(size, get, put):
        update = jnp.dot(
            lhs[: GROUPS * size, : 8 * KEEP], inverse[...], preferred_element_type=jnp.float32
        )
        for i in range(GROUPS):
            cols = pl.ds(column_group(i) * GW, GW)
            rest = get(cols).astype(jnp.float32) - update[i * size : (i + 1) * size]
            put(cols, rest.astype(jnp.bfloat16))

    def new_rows(q):
        arrive(("mean", q))
        if not mom_ready:
            mom_load.wait()
            mom_ready.append(q)
        start, size = CHUNKS[q]
        rows = pl.ds(start, size)
        for i in range(GROUPS):
            cols = pl.ds(column_group(i) * 4 * KEEP, 4 * KEEP)
            avg = means[i // 2, i % 2, rows].astype(jnp.float32)
            fresh = 0.9 * mom[rows, cols] + avg
            new_mom[rows, cols] = fresh
            step = (avg + 0.9 * fresh).astype(jnp.bfloat16)
            if q == 0:
                steps[0, 0, :, cols] = step
            else:
                lhs[pl.ds(i * size, size), : 4 * KEEP] = step
                lhs[pl.ds(i * size, size), 4 * KEEP : 8 * KEEP] = step

        def put(cols, value):
            T[0, 0, rows, cols] = value

        if q > 0:
            subtract(size, lambda cols: gbuf[rows, cols], put)
        return []

    mom_ready = []

    def load_raw(q):
        raw_load.wait()
        return []

    def finish_raw(part):
        parity = part // 2
        if part == 0:
            arrive(*[key for key in flying if key[1] in ("raw", 0) and key[0] not in SHARES])
            for copy in raw_copies:
                copy.wait_send()
        if part == 2:
            arrive(*[key for key in flying if key[1] in ("raw", 0)])
        size = CHUNKS[0][1]

        def one(n, carry):
            slot = (part % 2) * 4 + n
            for i in range(GROUPS):
                cols = pl.ds(column_group(i) * 4 * KEEP, 4 * KEEP)
                step = steps[parity, slot, :, cols]
                lhs[pl.ds(i * size, size), : 4 * KEEP] = step
                lhs[pl.ds(i * size, size), 4 * KEEP : 8 * KEEP] = step

            def put(cols, value):
                T[parity, slot, first, cols] = value

            subtract(size, lambda cols: T[parity, slot, first, cols], put)
            return carry

        lax.fori_loop(0, 4, one, 0)
        return []

    def pass_on(q, name):
        a1, a2, b = SPLIT[q]
        a = a1 + a2
        width = a + NZ * b
        buf = steps if q == 0 else T
        rows = pl.ds(0, CHUNKS[0][1]) if q == 0 else first if q == "raw" else pl.ds(*CHUNKS[q])
        odd = 0 if q == "raw" else q % 2
        p, p0, p1 = pl.ds(0, a1), pl.ds(0, a1 // 2), pl.ds(a1 // 2, a1 // 2)
        s, s0, s1 = pl.ds(a1, a2), pl.ds(a1, a2 // 2), pl.ds(a1 + a2 // 2, a2 // 2)

        def strip(k):
            return pl.ds(pl.multiple_of(a + zi(k) * b, 128), b)

        def send(slot, to_slot, cols, to, landing=None):
            return remote(
                buf.at[0, slot, rows, cols], buf.at[0, to_slot, rows, cols], to,
                None if landing is None else buf.at[0, to_slot, rows, landing],
            )

        def share(slot, cols):
            return [remote(buf.at[0, slot, rows, cols], buf.at[1, slot, rows, cols], sibling)]

        near, away = pl.ds(1, 3), pl.ds(5, 3)
        others = pl.ds(1, 7)
        if name == "ox1":
            return [send(0, 4, p0, right), send(0, 4, p1, left)]
        if name == "oy":
            return [send(0, 3, p, up), send(0, 1, p, down)]
        if name == "od":
            return share(0, pl.ds(0, width))
        if name == "y2":
            arrive(("oy", q))
            return [send(3, 2, p0, up), send(1, 2, p1, down)]
        if name == "x2a":
            arrive(("oy", q))
            return [send(i, i + 4, h, to) for i in (1, 3) for h, to in ((p0, right), (p1, left))]
        if name == "x2b":
            arrive(("y2", q))
            return [send(2, 6, p0, right), send(2, 6, p1, left)]
        if name == "d1":
            arrive(("oy", q), ("y2", q))
            return share(near, p)
        if name == "d2":
            arrive(("ox1", q), ("x2a", q), ("x2b", q))
            return share(pl.ds(4, 4), p)
        if name == "ox2":
            return [send(0, 4, s0, right), send(0, 4, s1, left)]
        if name == "ay0":
            return [send(0, 3, s, up), send(0, 1, s, down)]
        if name == "ay1":
            arrive(("ox2", q))
            return [send(4, 7, s, up), send(4, 5, s, down)]
        if name == "ay2":
            arrive(("ay0", q), ("ay1", q))
            return [send(3, 2, s, up), send(5, 6, s, down)]
        if name == "d3":
            arrive(("ay2", q))
            return share(others, s)
        mine = strip(0)
        if name == "oyB":
            return [send(0, 3, mine, up), send(0, 1, mine, down)]
        if name == "oxB":
            return [send(0, 4, mine, right if odd else left)]
        if name == "yB2":
            arrive(("oyB", q))
            return [send(1, 2, mine, down) if odd else send(3, 2, mine, up)]
        if name == "xB2":
            arrive(("yB2", q))
            return [send(near, away, mine, left if odd else right)]
        if name == "d4":
            arrive(("z3", q))
            return share(others, pl.ds(a, width - a))
        hop = int(name[1])
        arrive(*((("xB2", q), ("oxB", q)) if hop == 0 else (("z%d" % (hop - 1), q),)))
        onward = [
            (strip(-hop), ahead, strip(-hop - 1)),
            (strip(hop), behind, strip(hop + 1)),
        ]
        if hop == 3:
            onward = onward[odd : odd + 1]
        return [send(others, others, cols, to, landing) for cols, to, landing in onward]

    raw_copies = []
    compute = {"coef": coef, "sum": partial_sum, "mean": mean, "rows": new_rows,
               "load": load_raw, "fix": finish_raw}
    for name, q in ORDER:
        before = len(all_copies)
        if name in compute:
            flying[name, q] = compute[name](q)
        else:
            flying[name, q] = pass_on(q, name)
        if q == "raw":
            raw_copies += all_copies[before:]
    arrive(*list(flying))
    for copy in all_copies:
        if not any(copy is other for other in raw_copies):
            copy.wait_send()


def place_kernel(T, mom, params, new_mom, sem):
    x, y, z, c = here()
    copies = []
    for p in range(2):
        for dy in range(4):
            for dx in range(2):
                slot = dx * 4 + dy
                shard = (
                    lax.rem(y + dy, NY) * 4 + lax.rem(x + dx, 2) * 2 + lax.rem(c + p, 2)
                )
                for part in range(PIECES):
                    size = SHARD // PIECES
                    rows = pl.ds(pl.multiple_of(shard * SHARD + part * size, size), size)
                    copies.append(
                        pltpu.make_async_copy(
                            T.at[p, slot, pl.ds(part * size, size)], params.at[rows],
                            sem.at[len(copies)],
                        )
                    )
    copies.append(pltpu.make_async_copy(mom, new_mom, sem.at[len(copies)]))
    for copy in copies:
        copy.start()
    for copy in copies:
        copy.wait()


def on_device(local_params, global_params, momentum, kept):
    lanes = kept[None, :]
    bf16, f32 = jnp.bfloat16, jnp.float32
    anywhere = pl.BlockSpec(memory_space=pl.ANY)
    in_vmem = pl.BlockSpec(memory_space=pltpu.VMEM)
    T, mom = pl.pallas_call(
        outer_kernel,
        out_shape=(pltpu.VMEM((2, 8, SHARD, D), bf16), pltpu.VMEM((SHARD, D // 4), f32)),
        in_specs=[anywhere, anywhere, anywhere, in_vmem],
        out_specs=(in_vmem, in_vmem),
        scratch_shapes=[
            pltpu.VMEM((SHARD, D), bf16),
            pltpu.VMEM((SHARD, D), bf16),
            pltpu.VMEM((SHARD, D // 4), f32),
            pltpu.VMEM((2, 8, CHUNKS[0][1], D // 4), bf16),
            pltpu.VMEM((GW, 8 * KEEP), bf16),
            pltpu.VMEM((8 * KEEP, GW), bf16),
            pltpu.VMEM((GROUPS * max(size for _, size in CHUNKS), GW), bf16),
            pltpu.VMEM((NZ, 2, SHARD, 4 * KEEP), bf16),
            pltpu.VMEM((NZ, 2, SHARD, 4 * KEEP), bf16),
            pltpu.VMEM((2, SHARD, 4 * KEEP), bf16),
            pltpu.VMEM((2, SHARD, 4 * KEEP), bf16),
            pltpu.VMEM((NZ, 2, SHARD, 4 * KEEP), bf16),
            pltpu.SemaphoreType.DMA((2 * NQ + 2,)),
            pltpu.SemaphoreType.DMA((SEMAPHORES,)),
            pltpu.SemaphoreType.DMA((SEMAPHORES,)),
        ],
        compiler_params=pltpu.CompilerParams(
            collective_id=0, has_side_effects=True, vmem_limit_bytes=VMEM
        ),
    )(local_params, global_params, momentum, lanes)
    return pl.pallas_call(
        place_kernel,
        out_shape=(
            jax.ShapeDtypeStruct((ROWS, D), bf16),
            jax.ShapeDtypeStruct((SHARD, D // 4), f32),
        ),
        in_specs=[in_vmem, in_vmem],
        out_specs=(anywhere, anywhere),
        scratch_shapes=[pltpu.SemaphoreType.DMA((16 * PIECES + 1,))],
        compiler_params=pltpu.CompilerParams(vmem_limit_bytes=VMEM),
    )(
        pltpu.with_memory_space_constraint(T, pltpu.VMEM),
        pltpu.with_memory_space_constraint(mom, pltpu.VMEM),
    )


def solution(mesh):
    in_specs = (P("replica", "fsdp", None), P("fsdp", None), P("fsdp", None), P())
    out_specs = (P(), P("fsdp", None))
    return jax.shard_map(
        on_device, mesh=mesh, in_specs=in_specs, out_specs=out_specs, check_vma=False
    )
```
